32 devices in a mesh: fsdp: 8 (over z, core), seq: 4 (over y, x).
Axes of the slice: x: 2, y: 2, z: 4, core: 2. Of those that a mesh axis runs over, the one named last changes fastest.
Arguments:
- inputs: bfloat16 [8, 1024, 1024], P('fsdp', 'seq'), may hold values from -6 to 6
- segments: int32 [8, 1024], P('fsdp'), may hold values from 0 to 1, as said below
- cotangent: bfloat16 [8, 1024, 1024], P('fsdp', 'seq'), may hold values from -6 to 6
- first_gain: bfloat16 [1024], P(('fsdp', 'seq')), may hold values from 0.5 to 1.5
- first_shift: bfloat16 [1024], P(('fsdp', 'seq')), may hold values from -2 to 2
- qkv_weight: bfloat16 [1024, 3072], P(('fsdp', 'seq')), may hold values from -0.1875 to 0.1875
- query_bias: bfloat16 [1024], P(('fsdp', 'seq')), may hold values from -3 to 3
- value_bias: bfloat16 [1024], P(('fsdp', 'seq')), may hold values from -3 to 3
- output_weight: bfloat16 [1024, 1024], P(('fsdp', 'seq')), may hold values from -1 to 1
- output_bias: bfloat16 [1024], P(('fsdp', 'seq')), may hold values from -3 to 3
- second_gain: bfloat16 [1024], P(('fsdp', 'seq')), may hold values from 0.5 to 1.5
- second_shift: bfloat16 [1024], P(('fsdp', 'seq')), may hold values from -2 to 2
- expand_weight: bfloat16 [1024, 4096], P(('fsdp', 'seq')), may hold values from -0.1875 to 0.1875
- expand_bias: bfloat16 [4096], P(('fsdp', 'seq')), may hold values from -3 to 3
- shrink_weight: bfloat16 [4096, 1024], P(('fsdp', 'seq')), may hold values from -0.09375 to 0.09375
- shrink_bias: bfloat16 [1024], P(('fsdp', 'seq')), may hold values from -3 to 3
Outputs:
- outputs: bfloat16 [8, 1024, 1024], P('fsdp', 'seq')
- input_grad: bfloat16 [8, 1024, 1024], P('fsdp', 'seq')
- first_gain_grad: float32 [1024], P(('fsdp', 'seq'))
- first_shift_grad: float32 [1024], P(('fsdp', 'seq'))
- qkv_weight_grad: float32 [1024, 3072], P(('fsdp', 'seq'))
- query_bias_grad: float32 [1024], P(('fsdp', 'seq'))
- value_bias_grad: float32 [1024], P(('fsdp', 'seq'))
- output_weight_grad: float32 [1024, 1024], P(('fsdp', 'seq'))
- output_bias_grad: float32 [1024], P(('fsdp', 'seq'))
- second_gain_grad: float32 [1024], P(('fsdp', 'seq'))
- second_shift_grad: float32 [1024], P(('fsdp', 'seq'))
- expand_weight_grad: float32 [1024, 4096], P(('fsdp', 'seq'))
- expand_bias_grad: float32 [4096], P(('fsdp', 'seq'))
- shrink_weight_grad: float32 [4096, 1024], P(('fsdp', 'seq'))
- shrink_bias_grad: float32 [1024], P(('fsdp', 'seq'))
The draws below stay inside these ranges and needn't reach their ends.
Inputs may be any that keep to these rules, and one draw needn't show every extreme that they name: `segments`: along each sequence the numbers start at 0 and rise by 0 or 1 from one token to the next; every sequence holds exactly 2 documents; in each aligned block of 1 sequence, the first document of one sequence covers all but the last 256 tokens or fewer.
All inputs are finite; a program needn't handle non-finite values.
Results may differ from the reference program's by a relative error of at most 0.012.
Values may be sent and summed in bfloat16 or wider, within the bound.
A program may use at most 256 MiB of HBM per device.

```python
import jax
import jax.numpy as jnp
from jax import lax

D = 1024
HEADS = 16
HEAD_DIM = 64
FF = 4096
SEQ_LEN = 1024
GROUP = 256
SEQS = 1
SEQ_TOTAL = 8
DOCS = 2


def draw_segments(key, part):
    key = jax.random.fold_in(key, 5)
    mark_key, pick_key = jax.random.split(key)
    documents = DOCS
    row_keys = jax.random.split(mark_key, SEQ_TOTAL)
    places = jnp.arange(SEQ_LEN).astype(jnp.int32)

    def bounds_of(row_key):
        spread_key, tail_key = jax.random.split(row_key)
        order = jax.random.permutation(spread_key, SEQ_LEN - 1).astype(jnp.int32) + 1
        tail = jax.random.permutation(tail_key, GROUP - 1).astype(jnp.int32) + (SEQ_LEN - GROUP + 1)
        return (order[:documents - 1], tail[:documents - 1])
    spread_bounds, tail_bounds = jax.vmap(bounds_of)(row_keys)
    picks = jax.random.randint(pick_key, (SEQ_TOTAL // SEQS,), 0, SEQS)
    rows = jnp.arange(SEQ_TOTAL)
    spanning = rows % SEQS == picks[rows // SEQS]
    chosen = jnp.where(spanning[:, None], tail_bounds, spread_bounds)
    marks = jnp.any(places[None, :, None] == chosen[:, None, :], axis=2)
    return jnp.cumsum(marks.astype(jnp.int32), axis=1).astype(jnp.int32)


def steps_of(stream_key, dims, cuts, least, high):
    level, own = 1.0, jax.random.fold_in(stream_key, 6)
    for axis_at, shards_of in cuts:
        steps = jnp.exp(jax.random.uniform(jax.random.fold_in(own, axis_at), (shards_of,), jnp.float32, least / len(cuts), high / len(cuts)))
        level = level * jnp.repeat(steps, dims[axis_at] // shards_of).reshape([-1 if axis == axis_at else 1 for axis in range(len(dims))])
    return level


def bell_draw(own_key, dims, deviation, limit, cuts=(), dtype=jnp.bfloat16):
    values = deviation * jax.random.normal(own_key, dims, jnp.float32)
    if cuts:
        values = values * steps_of(own_key, dims, cuts, -0.22, 0.18)
    return jnp.clip(values, -limit, limit).astype(dtype)


def setup_inputs(seed: int = 0) -> dict:
    seeds = jax.random.split(jax.random.key(seed), 17)
    inputs = bell_draw(seeds[0], (SEQ_TOTAL, SEQ_LEN, D), 1.0, 6.0, ((0, 8), (1, 4)))
    segments = draw_segments(jax.random.fold_in(seeds[16], 71), 0)
    cotangent = bell_draw(seeds[2], (SEQ_TOTAL, SEQ_LEN, D), 1.0, 6.0, ((0, 8), (1, 4)))
    first_gain = jnp.clip(1.0 + 0.1 * jax.random.normal(seeds[3], (D,), jnp.float32), 0.5, 1.5).astype(jnp.bfloat16)
    first_shift = bell_draw(seeds[4], (D,), 0.3, 2.0, ((0, 32),))
    qkv_weight = bell_draw(seeds[5], (D, 3 * D), D ** -0.5, 0.1875, ((0, 32),))
    query_bias = bell_draw(seeds[6], (D,), 0.5, 3.0, ((0, 32),))
    value_bias = bell_draw(seeds[7], (D,), 0.5, 3.0, ((0, 32),))
    output_weight = bell_draw(seeds[8], (D, D), (D // 32) ** -0.5, 1.0, ((0, 32),))
    output_bias = bell_draw(seeds[9], (D,), 0.5, 3.0, ((0, 32),))
    second_gain = jnp.clip(1.0 + 0.1 * jax.random.normal(seeds[10], (D,), jnp.float32), 0.5, 1.5).astype(jnp.bfloat16)
    second_shift = bell_draw(seeds[11], (D,), 0.3, 2.0, ((0, 32),))
    expand_weight = bell_draw(seeds[12], (D, FF), D ** -0.5, 0.1875, ((0, 32),))
    expand_bias = bell_draw(seeds[13], (FF,), 0.5, 3.0, ((0, 32),))
    shrink_weight = bell_draw(seeds[14], (FF, D), FF ** -0.5, 0.09375, ((0, 32),))
    shrink_bias = bell_draw(seeds[15], (D,), 0.5, 3.0, ((0, 32),))
    return {"inputs": inputs, "segments": segments, "cotangent": cotangent, "first_gain": first_gain, "first_shift": first_shift, "qkv_weight": qkv_weight, "query_bias": query_bias, "value_bias": value_bias, "output_weight": output_weight, "output_bias": output_bias, "second_gain": second_gain, "second_shift": second_shift, "expand_weight": expand_weight, "expand_bias": expand_bias, "shrink_weight": shrink_weight, "shrink_bias": shrink_bias}


@jax.custom_vjp
def low(v):
    return lax.optimization_barrier(v.astype(jnp.bfloat16)).astype(jnp.float32)

@jax.custom_vjp
def low_back(v):
    return v

def low_keep(v):
    return (low(v), None)

def low_pass(kept, grad):
    return (grad,)

def back_keep(v):
    return (v, None)

def back_low(kept, grad):
    return (low(grad),)
low.defvjp(low_keep, low_pass)
low_back.defvjp(back_keep, back_low)

def layer_norm(values, gain, shift):
    centre = values - lax.optimization_barrier(jnp.mean(values, axis=-1, keepdims=True))
    spread = lax.optimization_barrier(jnp.mean(centre * centre, axis=-1, keepdims=True))
    return centre * lax.rsqrt(spread + 1e-05) * gain + shift

def gelu_tanh(values):
    return 0.5 * values * (1.0 + jnp.tanh(0.7978845608028654 * (values + 0.044715 * values * values * values)))

def product(left, right):
    return jnp.dot(left, right, precision=lax.Precision.HIGHEST)

def sequence_layer(params, tokens, segment_row):
    first_gain, first_shift, qkv_weight, query_bias, value_bias, output_weight, output_bias, second_gain, second_shift, expand_weight, expand_bias, shrink_weight, shrink_bias = params
    length = tokens.shape[0]
    normed = low(layer_norm(tokens, first_gain, first_shift))
    joined = product(normed, qkv_weight)
    queries = low(low_back(joined[:, :D] + query_bias))
    keys = low(low_back(joined[:, D:2 * D]))
    values = low(low_back(joined[:, 2 * D:] + value_bias))
    places = jnp.arange(length)
    allowed = (places[None, :] <= places[:, None]) & (segment_row[None, :] == segment_row[:, None])

    def one_head(item):
        head_query, head_key, head_value = item
        scores = low_back(product(head_query, head_key.T) * 0.125)
        scores = jnp.where(allowed, scores, -1e+30)
        largest = lax.optimization_barrier(jnp.max(scores, axis=-1, keepdims=True))
        weights = jnp.exp(scores - largest)
        weights = weights / lax.optimization_barrier(jnp.sum(weights, axis=-1, keepdims=True))
        return product(low(weights), head_value)

    def split_heads(block):
        return block.reshape(length, HEADS, HEAD_DIM).transpose(1, 0, 2)
    mixed = lax.map(jax.checkpoint(one_head), (split_heads(queries), split_heads(keys), split_heads(values)))
    mixed = low(low_back(mixed.transpose(1, 0, 2).reshape(length, D)))
    branch = low_back(product(mixed, output_weight) + output_bias)
    middle = tokens + branch
    second = low(layer_norm(middle, second_gain, second_shift))
    hidden_pre = low_back(product(second, expand_weight) + expand_bias)
    hidden = low(gelu_tanh(hidden_pre))
    shrink = low_back(product(hidden, shrink_weight) + shrink_bias)
    return middle + shrink

def reference(inputs, segments, cotangent, first_gain, first_shift, qkv_weight, query_bias, value_bias, output_weight, output_bias, second_gain, second_shift, expand_weight, expand_bias, shrink_weight, shrink_bias):
    params = tuple((w.astype(jnp.float32) for w in (first_gain, first_shift, qkv_weight, query_bias, value_bias, output_weight, output_bias, second_gain, second_shift, expand_weight, expand_bias, shrink_weight, shrink_bias)))

    def step(totals, item):
        tokens, segment_row, grad_row = item

        def layer_of(weights, values):
            return sequence_layer(weights, values, segment_row)
        result, pull = jax.vjp(layer_of, params, tokens.astype(jnp.float32))
        grad_params, grad_tokens = pull(grad_row.astype(jnp.float32))
        totals = jax.tree.map(lambda a, b: a + b, totals, grad_params)
        return (totals, (result.astype(jnp.bfloat16), grad_tokens.astype(jnp.bfloat16)))
    zeros = jax.tree.map(jnp.zeros_like, params)
    totals, (results, grads) = lax.scan(step, zeros, (inputs, segments, cotangent))
    return (results, grads) + tuple(totals)
```

```python
import functools
import math

import jax
import jax.numpy as jnp
from jax import lax
from jax.experimental import pallas as pl
from jax.experimental.pallas import tpu as pltpu
from jax.sharding import PartitionSpec as P

HEAD_DIM = 64

BLOCK_ROWS = 32
BLOCK_COLUMNS = 1024
MESH = pl.DeviceIdType.MESH


def lattice(group_count, place_count):
    side = math.isqrt(place_count)
    return {"z": group_count // 2, "core": 2, "y": place_count // side, "x": side}


def here(sizes):
    group, place = lax.axis_index("fsdp"), lax.axis_index("seq")
    return {
        "z": group // 2,
        "core": lax.rem(group, 2),
        "y": place // sizes["x"],
        "x": lax.rem(place, sizes["x"]),
    }


def moved(me, sizes, dim, step):
    other = dict(me)
    other[dim] = lax.rem(me[dim] + step + sizes[dim], sizes[dim])
    return other


def device_of(at, sizes):
    return {"fsdp": at["z"] * 2 + at["core"], "seq": at["y"] * sizes["x"] + at["x"]}


def greet(me, sizes, dims):
    barrier = pltpu.get_barrier_semaphore()
    count = 0
    for dim in dims:
        for step in range(1, sizes[dim]):
            pl.semaphore_signal(
                barrier,
                inc=1,
                device_id=device_of(moved(me, sizes, dim, step), sizes),
                device_id_type=MESH,
            )
            count += 1
    pl.semaphore_wait(barrier, count)


def pieces_of(shapes, rows_most, columns_most):
    pieces = []
    for item, (rows, columns) in enumerate(shapes):
        high, wide = min(rows, rows_most), min(columns, columns_most)
        if rows % high:
            high = rows
        if columns % wide:
            wide = columns
        for row in range(0, rows, high):
            for column in range(0, columns, wide):
                pieces.append((item, row, column, high, wide))
    return pieces


def slots_of(dims, sizes):
    return {
        dim: sum(sizes[other] - 1 for other in dims[: at]) for at, dim in enumerate(dims)
    }, sum(sizes[dim] - 1 for dim in dims)


def gather_kernel(dims, sizes, pieces, count, *refs):
    ins, outs = refs[:count], refs[count : 2 * count]
    send_sem, recv_sem, own_sem = refs[2 * count :]
    me = here(sizes)
    greet(me, sizes, dims)
    slot, _ = slots_of(dims, sizes)
    own = [
        pltpu.make_async_copy(
            ins[item], outs[item].at[tuple(me[dim] for dim in dims)], own_sem.at[item]
        )
        for item in range(count)
    ]
    for copy in own:
        copy.start()
    own_waited = set()

    def order_of(number):
        across = ("x", "y") if number % 2 == 0 else ("y", "x")
        return [dim for dim in ("z",) + across + ("core",) if dim in dims]

    def region(number, stage, at):
        item, row, column, high, wide = pieces[number]
        done = order_of(number)[:stage]
        index = tuple(slice(None) if dim in done else at[dim] for dim in dims)
        return outs[item].at[index + (pl.ds(row, high), pl.ds(column, wide))]

    def copy_of(number, stage, step, source, target, device):
        place = slot[order_of(number)[stage]] + step - 1
        return pltpu.make_async_remote_copy(
            src_ref=source,
            dst_ref=target,
            send_sem=send_sem.at[number, place],
            recv_sem=recv_sem.at[number, place],
            device_id=device_of(device, sizes),
            device_id_type=MESH,
        )

    def receive(number, stage):
        dim = order_of(number)[stage]
        for step in range(1, sizes[dim]):
            giver = moved(me, sizes, dim, -step)
            landed = region(number, stage, giver)
            copy_of(number, stage, step, landed, landed, giver).wait_recv()

    sent = []
    depth = len(dims)
    for tick in range(len(pieces) + depth):
        for stage in range(depth, -1, -1):
            number = tick - stage
            if not 0 <= number < len(pieces):
                continue
            item, row, column, high, wide = pieces[number]
            if stage > 0:
                receive(number, stage - 1)
            if stage == depth:
                continue
            if stage == 1 and item not in own_waited:
                own[item].wait()
                own_waited.add(item)
            dim = order_of(number)[stage]
            target = region(number, stage, me)
            source = target
            if stage == 0:
                source = ins[item].at[pl.ds(row, high), pl.ds(column, wide)]
            for step in range(1, sizes[dim]):
                copy = copy_of(
                    number, stage, step, source, target, moved(me, sizes, dim, step)
                )
                copy.start()
                sent.append(copy)
    for copy in sent:
        copy.wait_send()
    for item in range(count):
        if item not in own_waited:
            own[item].wait()


def gather_blocks(shards, dims, sizes, pieces, identity):
    count = len(shards)
    _, total = slots_of(dims, sizes)
    front = tuple(sizes[dim] for dim in dims)
    return pl.pallas_call(
        functools.partial(gather_kernel, dims, sizes, pieces, count),
        out_shape=[jax.ShapeDtypeStruct(front + s.shape, s.dtype) for s in shards],
        in_specs=[pl.BlockSpec(memory_space=pl.ANY)] * count,
        out_specs=[pl.BlockSpec(memory_space=pl.ANY)] * count,
        scratch_shapes=[
            pltpu.SemaphoreType.DMA((len(pieces), total)),
            pltpu.SemaphoreType.DMA((len(pieces), total)),
            pltpu.SemaphoreType.DMA((count,)),
        ],
        compiler_params=pltpu.CompilerParams(collective_id=identity, has_side_effects=True),
    )(*shards)


def scatter_plan(number, dims):
    across = ("x", "y") if number % 2 == 0 else ("y", "x")
    return [dim for dim in ("core",) + across + ("z",) if dim in dims]


def landing_shape(number, stage, dims, sizes, piece):
    order = scatter_plan(number, dims)
    left = tuple(sizes[dim] for dim in dims if dim not in order[: stage + 1])
    return (sizes[order[stage]] - 1,) + left + piece[3:]


def scatter_kernel(dims, sizes, pieces, count, *refs):
    ins, outs = refs[:count], refs[count : 2 * count]
    rest = list(refs[2 * count :])
    depth = len(dims)
    sums = rest[: len(pieces)]
    landing = [
        rest[len(pieces) + number * depth : len(pieces) + (number + 1) * depth]
        for number in range(len(pieces))
    ]
    send_sem, recv_sem, load_sem = rest[-3:]
    me = here(sizes)
    greet(me, sizes, dims)
    slot, _ = slots_of(dims, sizes)
    held = [dim for dim in dims if dim != "core"]

    def window(number, at):
        item, row, column, high, wide = pieces[number]
        index = tuple(at[dim] if dim == "core" else slice(None) for dim in dims)
        return ins[item].at[index + (pl.ds(row, high), pl.ds(column, wide))]

    loads = []
    for number in range(len(pieces)):
        load = pltpu.make_async_copy(window(number, me), sums[number], load_sem.at[number])
        load.start()
        loads.append(load)

    sent = []

    def copies(number, stage):
        dim = scatter_plan(number, dims)[stage]
        done = scatter_plan(number, dims)[:stage]
        made = []
        for step in range(1, sizes[dim]):
            peer = moved(me, sizes, dim, step)
            if dim == "core":
                source = window(number, peer)
            else:
                index = tuple(
                    peer[other] if other == dim else me[other] if other in done else slice(None)
                    for other in held
                )
                source = sums[number].at[index]
            place = slot[dim] + step - 1
            made.append(
                pltpu.make_async_remote_copy(
                    src_ref=source,
                    dst_ref=landing[number][stage].at[step - 1],
                    send_sem=send_sem.at[number, place],
                    recv_sem=recv_sem.at[number, place],
                    device_id=device_of(peer, sizes),
                    device_id_type=MESH,
                )
            )
        return made

    def reduce(number, stage):
        item, row, column, high, wide = pieces[number]
        order = scatter_plan(number, dims)
        left = [dim for dim in held if dim not in order[: stage + 1]]
        blocks = math.prod(sizes[dim] for dim in left)
        tile = min(high, BLOCK_ROWS)
        bands = high // tile

        def body(turn, carry):
            band = pl.ds(pl.multiple_of(lax.rem(turn, bands) * tile, tile), tile)
            block = turn // bands
            at = {}
            for dim in reversed(left):
                at[dim] = lax.rem(block, sizes[dim])
                block = block // sizes[dim]
            spot = tuple(at[dim] if dim in left else me[dim] for dim in held)
            value = sums[number][spot + (band, slice(None))].astype(jnp.float32)
            for step in range(1, sizes[order[stage]]):
                arrived = landing[number][stage][
                    (step - 1,) + tuple(at[dim] for dim in left) + (band, slice(None))
                ]
                value = value + arrived.astype(jnp.float32)
            if stage == depth - 1:
                start = pl.multiple_of(row + lax.rem(turn, bands) * tile, tile)
                outs[item][pl.ds(start, tile), pl.ds(column, wide)] = value
            else:
                sums[number][spot + (band, slice(None))] = value.astype(jnp.bfloat16)
            return carry

        lax.fori_loop(0, blocks * bands, body, 0)

    flights = {}
    for tick in range(len(pieces) + depth):
        for stage in range(depth, -1, -1):
            number = tick - stage
            if not 0 <= number < len(pieces):
                continue
            if stage > 0:
                if stage == 1 and loads[number] is not None:
                    loads[number].wait()
                    loads[number] = None
                for copy in flights[number, stage - 1]:
                    copy.wait_recv()
                reduce(number, stage - 1)
            if stage < depth:
                if stage == 0 and "core" not in dims:
                    loads[number].wait()
                    loads[number] = None
                made = copies(number, stage)
                for copy in made:
                    copy.start()
                    sent.append(copy)
                flights[number, stage] = made
    for copy in sent:
        copy.wait_send()


def scatter_blocks(blocks, dims, sizes, pieces, identity, limit):
    count = len(blocks)
    _, total = slots_of(dims, sizes)
    held = tuple(sizes[dim] for dim in dims if dim != "core")
    shapes = [b.shape[len(dims) :] for b in blocks]
    scratch = [pltpu.VMEM(held + piece[3:], jnp.bfloat16) for piece in pieces]
    for number, piece in enumerate(pieces):
        for stage in range(len(dims)):
            scratch.append(
                pltpu.VMEM(landing_shape(number, stage, dims, sizes, piece), jnp.bfloat16)
            )
    return pl.pallas_call(
        functools.partial(scatter_kernel, dims, sizes, pieces, count),
        out_shape=[jax.ShapeDtypeStruct(shape, jnp.float32) for shape in shapes],
        in_specs=[pl.BlockSpec(memory_space=pl.ANY)] * count,
        out_specs=[pl.BlockSpec(memory_space=pltpu.VMEM)] * count,
        scratch_shapes=scratch
        + [
            pltpu.SemaphoreType.DMA((len(pieces), total)),
            pltpu.SemaphoreType.DMA((len(pieces), total)),
            pltpu.SemaphoreType.DMA((len(pieces),)),
        ],
        compiler_params=pltpu.CompilerParams(
            collective_id=identity, has_side_effects=True, vmem_limit_bytes=limit
        ),
    )(*blocks)


ALL_DIMS = ("z", "core", "y", "x")
SEQ_DIMS = ("y", "x")


def tall(rows, columns):
    if rows % 16 == 0:
        return rows, columns
    return 16, rows * columns // 16


def gather_weights(matrices, vectors, sizes):
    count = math.prod(sizes[dim] for dim in ALL_DIMS)
    packed = jnp.concatenate(vectors)
    packed = jnp.pad(packed, (0, 2048 - packed.size)).reshape(16, 128)
    shards = [packed] + [m.reshape(tall(*m.shape)) for m in matrices]
    pieces = pieces_of([s.shape for s in shards], BLOCK_ROWS, BLOCK_COLUMNS)
    whole = gather_blocks(shards, ALL_DIMS, sizes, pieces, 0)
    flat = whole[0].reshape(count, 2048)
    parts, offset = [], 0
    for vector in vectors:
        parts.append(flat[:, offset : offset + vector.size].reshape(count * vector.size))
        offset += vector.size
    full = [
        w.reshape(count * m.shape[0], m.shape[1]) for w, m in zip(whole[1:], matrices)
    ]
    return full, parts


def scatter_grads(matrices, vectors, sizes):
    count = math.prod(sizes[dim] for dim in ALL_DIMS)
    front = tuple(sizes[dim] for dim in ALL_DIMS)
    packed = jnp.concatenate([v.reshape(count, -1) for v in vectors], axis=1)
    packed = jnp.pad(packed, ((0, 0), (0, 2048 - packed.shape[1]))).astype(jnp.bfloat16)
    blocks = [packed.reshape(front + (16, 128))]
    for matrix in matrices:
        shape = tall(matrix.shape[0] // count, matrix.shape[1])
        blocks.append(matrix.reshape(front + shape))
    pieces = pieces_of([b.shape[4:] for b in blocks], BLOCK_ROWS, BLOCK_COLUMNS)
    owned = scatter_blocks(blocks, ALL_DIMS, sizes, pieces, 1, 52 * 1024 * 1024)
    flat = owned[0].reshape(2048)
    parts, offset = [], 0
    for vector in vectors:
        part = vector.size // count
        parts.append(flat[offset : offset + part])
        offset += part
    full = [
        o.reshape(m.shape[0] // count, m.shape[1]) for o, m in zip(owned[1:], matrices)
    ]
    return full, parts


def gather_sequence(arrays, sizes):
    seqs, group, width = arrays[0].shape
    count = sizes["x"] * sizes["y"]
    shards = [a.reshape(seqs * group, width) for a in arrays]
    pieces = pieces_of([s.shape for s in shards], seqs * group, 512)
    whole = gather_blocks(shards, SEQ_DIMS, sizes, pieces, 2)
    return [
        jnp.moveaxis(w.reshape(count, seqs, group, width), 0, 1).reshape(
            seqs, count * group, width
        )
        for w in whole
    ]


def scatter_sequence(arrays, sizes):
    seqs, length, width = arrays[0].shape
    count = sizes["x"] * sizes["y"]
    group = length // count
    front = (sizes["y"], sizes["x"])
    blocks = [
        jnp.moveaxis(a.reshape(seqs, count, group, width), 1, 0).reshape(
            front + (seqs * group, width)
        )
        for a in arrays
    ]
    pieces = pieces_of([b.shape[2:] for b in blocks], seqs * group, 512)
    owned = scatter_blocks(blocks, SEQ_DIMS, sizes, pieces, 3, 52 * 1024 * 1024)
    return [o.reshape(seqs, group, width) for o in owned]


def layer_norm(values, gain, shift):
    centre = values - jnp.mean(values, axis=-1, keepdims=True)
    spread = jnp.mean(centre * centre, axis=-1, keepdims=True)
    return centre * lax.rsqrt(spread + 1e-05) * gain + shift


def gelu_tanh(values):
    return (
        0.5
        * values
        * (1.0 + jnp.tanh(0.7978845608028654 * (values + 0.044715 * values * values * values)))
    )


def rows_product(left, right):
    return jnp.dot(left, right, preferred_element_type=jnp.float32)


def weight_grad(left, right):
    return lax.dot_general(
        left, right, (((0,), (0,)), ((), ())), preferred_element_type=jnp.float32
    )


def input_grad(left, right):
    return lax.dot_general(
        left, right, (((1,), (1,)), ((), ())), preferred_element_type=jnp.float32
    )


def column_sum(values):
    return jnp.sum(values.astype(jnp.float32), axis=0)


def masked_scores(queries, keys, allowed):
    scores = (
        jnp.einsum("bqhd,bkhd->bhqk", queries, keys, preferred_element_type=jnp.float32) * 0.125
    )
    return jnp.where(allowed, scores, -1e30)


def local(
    inputs,
    segments,
    cotangent,
    first_gain,
    first_shift,
    qkv_weight,
    query_bias,
    value_bias,
    output_weight,
    output_bias,
    second_gain,
    second_shift,
    expand_weight,
    expand_bias,
    shrink_weight,
    shrink_bias,
):
    sizes = lattice(lax.axis_size("fsdp"), lax.axis_size("seq"))
    matrices, vectors = gather_weights(
        (qkv_weight, output_weight, expand_weight, shrink_weight),
        (
            first_gain,
            first_shift,
            query_bias,
            value_bias,
            output_bias,
            second_gain,
            second_shift,
            expand_bias,
            shrink_bias,
        ),
        sizes,
    )
    qkv_full, output_full, expand_full, shrink_full = matrices
    forward_set = (
        vectors[0],
        vectors[1],
        qkv_full,
        vectors[2],
        vectors[3],
        output_full,
        vectors[4],
        vectors[5],
        vectors[6],
        expand_full,
        vectors[7],
        shrink_full,
        vectors[8],
    )
    seqs, group, width = inputs.shape
    length = segments.shape[1]
    heads = width // HEAD_DIM
    rows = seqs * group
    gain_first = forward_set[0].astype(jnp.float32)
    shift_first = forward_set[1].astype(jnp.float32)
    gain_second = forward_set[7].astype(jnp.float32)
    shift_second = forward_set[8].astype(jnp.float32)
    tokens = inputs.reshape(rows, width).astype(jnp.float32)
    acts_first = layer_norm(tokens, gain_first, shift_first).astype(jnp.bfloat16)
    joined = rows_product(acts_first, forward_set[2])
    query_rows = (joined[:, :width] + forward_set[3].astype(jnp.float32)).astype(jnp.bfloat16)
    key_local = joined[:, width : 2 * width].astype(jnp.bfloat16).reshape(seqs, group, width)
    value_local = (
        (joined[:, 2 * width :] + forward_set[4].astype(jnp.float32))
        .astype(jnp.bfloat16)
        .reshape(seqs, group, width)
    )
    key_all, value_all = gather_sequence((key_local, value_local), sizes)
    first_place = lax.axis_index("seq") * group
    query_segment = lax.dynamic_slice_in_dim(segments, first_place, group, 1)
    query_place = first_place + jnp.arange(group)
    key_place = jnp.arange(length)
    causal = key_place[None, :] <= query_place[:, None]
    allowed = (causal[None] & (query_segment[:, :, None] == segments[:, None, :]))[:, None]
    query_heads = query_rows.reshape(seqs, group, heads, HEAD_DIM)
    scores = masked_scores(query_heads, key_all.reshape(seqs, length, heads, HEAD_DIM), allowed)
    largest = jnp.max(scores, axis=-1, keepdims=True)
    expon = jnp.exp(scores - largest)
    total = jnp.sum(expon, axis=-1, keepdims=True)
    probs = (expon / total).astype(jnp.bfloat16)
    mixed = jnp.einsum(
        "bhqk,bkhd->bqhd",
        probs,
        value_all.reshape(seqs, length, heads, HEAD_DIM),
        preferred_element_type=jnp.float32,
    )
    mixed = mixed.reshape(rows, width).astype(jnp.bfloat16)
    middle = tokens + rows_product(mixed, forward_set[5]) + forward_set[6].astype(jnp.float32)
    acts_second = layer_norm(middle, gain_second, shift_second).astype(jnp.bfloat16)
    hidden_pre = rows_product(acts_second, forward_set[9]) + forward_set[10].astype(jnp.float32)
    acts_third = gelu_tanh(hidden_pre).astype(jnp.bfloat16)
    result = (
        middle + rows_product(acts_third, forward_set[11]) + forward_set[12].astype(jnp.float32)
    )
    outputs = result.astype(jnp.bfloat16).reshape(seqs, group, width)
    back_set = forward_set
    grad_out = cotangent.reshape(rows, width)
    grad_shrink = weight_grad(acts_third, grad_out)
    grad_shrink_bias = column_sum(grad_out)
    grad_hidden = input_grad(grad_out, back_set[11])
    gelu_value, gelu_pull = jax.vjp(gelu_tanh, hidden_pre)
    grad_pre = gelu_pull(grad_hidden)[0].astype(jnp.bfloat16)
    grad_expand = weight_grad(acts_second, grad_pre)
    grad_expand_bias = column_sum(grad_pre)
    grad_acts_second = input_grad(grad_pre, back_set[9])
    norm_value, second_pull = jax.vjp(
        layer_norm, middle, back_set[7].astype(jnp.float32), back_set[8].astype(jnp.float32)
    )
    grad_middle_norm, grad_gain_second, grad_shift_second = second_pull(grad_acts_second)
    grad_middle = grad_out.astype(jnp.float32) + grad_middle_norm
    grad_branch = grad_middle.astype(jnp.bfloat16)
    grad_output = weight_grad(mixed, grad_branch)
    grad_output_bias = column_sum(grad_branch)
    grad_mixed = (
        input_grad(grad_branch, back_set[5])
        .astype(jnp.bfloat16)
        .reshape(seqs, group, heads, HEAD_DIM)
    )
    key_back, value_back = key_all, value_all
    key_heads = key_back.reshape(seqs, length, heads, HEAD_DIM)
    value_heads = value_back.reshape(seqs, length, heads, HEAD_DIM)
    scores_again = masked_scores(query_heads, key_heads, allowed)
    probs_again = jnp.exp(scores_again - largest) / total
    grad_probs = jnp.einsum(
        "bqhd,bkhd->bhqk", grad_mixed, value_heads, preferred_element_type=jnp.float32
    )
    centred = jnp.sum(probs_again * grad_probs, axis=-1, keepdims=True)
    grad_scores = (probs_again * (grad_probs - centred)).astype(jnp.bfloat16)
    grad_query = (
        jnp.einsum("bhqk,bkhd->bqhd", grad_scores, key_heads, preferred_element_type=jnp.float32)
        * 0.125
    )
    key_terms = (
        jnp.einsum("bhqk,bqhd->bkhd", grad_scores, query_heads, preferred_element_type=jnp.float32)
        * 0.125
    )
    value_terms = jnp.einsum(
        "bhqk,bqhd->bkhd",
        probs_again.astype(jnp.bfloat16),
        grad_mixed,
        preferred_element_type=jnp.float32,
    )
    grad_key, grad_value = scatter_sequence(
        (
            key_terms.reshape(seqs, length, width).astype(jnp.bfloat16),
            value_terms.reshape(seqs, length, width).astype(jnp.bfloat16),
        ),
        sizes,
    )
    grad_joined = jnp.concatenate(
        [
            grad_query.reshape(rows, width),
            grad_key.reshape(rows, width),
            grad_value.reshape(rows, width),
        ],
        axis=1,
    ).astype(jnp.bfloat16)
    grad_qkv = weight_grad(acts_first, grad_joined)
    grad_query_bias = column_sum(grad_joined[:, :width])
    grad_value_bias = column_sum(grad_joined[:, 2 * width :])
    grad_acts_first = input_grad(grad_joined, back_set[2])
    first_value, first_pull = jax.vjp(
        layer_norm, tokens, back_set[0].astype(jnp.float32), back_set[1].astype(jnp.float32)
    )
    grad_tokens_norm, grad_gain_first, grad_shift_first = first_pull(grad_acts_first)
    grad_inputs = (grad_middle + grad_tokens_norm).astype(jnp.bfloat16).reshape(seqs, group, width)
    owned, parts = scatter_grads(
        tuple(
            grad.astype(jnp.bfloat16)
            for grad in (grad_qkv, grad_output, grad_expand, grad_shrink)
        ),
        (
            grad_gain_first,
            grad_shift_first,
            grad_query_bias,
            grad_value_bias,
            grad_output_bias,
            grad_gain_second,
            grad_shift_second,
            grad_expand_bias,
            grad_shrink_bias,
        ),
        sizes,
    )
    return (
        outputs,
        grad_inputs,
        parts[0],
        parts[1],
        owned[0],
        parts[2],
        parts[3],
        owned[1],
        parts[4],
        parts[5],
        parts[6],
        owned[2],
        parts[7],
        owned[3],
        parts[8],
    )


def solution(mesh):
    placed = (
        P("fsdp", "seq", None),
        P("fsdp", None),
        P("fsdp", "seq", None),
        P(("fsdp", "seq")),
        P(("fsdp", "seq")),
        P(("fsdp", "seq"), None),
        P(("fsdp", "seq")),
        P(("fsdp", "seq")),
        P(("fsdp", "seq"), None),
        P(("fsdp", "seq")),
        P(("fsdp", "seq")),
        P(("fsdp", "seq")),
        P(("fsdp", "seq"), None),
        P(("fsdp", "seq")),
        P(("fsdp", "seq"), None),
        P(("fsdp", "seq")),
    )
    return jax.shard_map(
        local,
        mesh=mesh,
        in_specs=placed,
        out_specs=(
            P("fsdp", "seq", None),
            P("fsdp", "seq", None),
            P(("fsdp", "seq")),
            P(("fsdp", "seq")),
            P(("fsdp", "seq"), None),
            P(("fsdp", "seq")),
            P(("fsdp", "seq")),
            P(("fsdp", "seq"), None),
            P(("fsdp", "seq")),
            P(("fsdp", "seq")),
            P(("fsdp", "seq")),
            P(("fsdp", "seq"), None),
            P(("fsdp", "seq")),
            P(("fsdp", "seq"), None),
            P(("fsdp", "seq")),
        ),
        check_vma=False,
    )
```

```python
import functools
import math

import jax
import jax.numpy as jnp
from jax import lax
from jax.experimental import pallas as pl
from jax.experimental.pallas import tpu as pltpu
from jax.sharding import PartitionSpec as P

HEAD_DIM = 64

BLOCK_ROWS = 32
BLOCK_COLUMNS = 1024
LAG = 2
MESH = pl.DeviceIdType.MESH


def lattice(group_count, place_count):
    side = math.isqrt(place_count)
    return {"z": group_count // 2, "core": 2, "y": place_count // side, "x": side}


def here(sizes):
    group, place = lax.axis_index("fsdp"), lax.axis_index("seq")
    return {
        "z": group // 2,
        "core": lax.rem(group, 2),
        "y": place // sizes["x"],
        "x": lax.rem(place, sizes["x"]),
    }


def moved(me, sizes, dim, step):
    other = dict(me)
    other[dim] = lax.rem(me[dim] + step + sizes[dim], sizes[dim])
    return other


def device_of(at, sizes):
    return {"fsdp": at["z"] * 2 + at["core"], "seq": at["y"] * sizes["x"] + at["x"]}


def greet(me, sizes, dims):
    barrier = pltpu.get_barrier_semaphore()
    count = 0
    for dim in dims:
        for step in range(1, sizes[dim]):
            pl.semaphore_signal(
                barrier,
                inc=1,
                device_id=device_of(moved(me, sizes, dim, step), sizes),
                device_id_type=MESH,
            )
            count += 1
    pl.semaphore_wait(barrier, count)


def pieces_of(shapes, rows_most, columns_most):
    pieces = []
    for item, (rows, columns) in enumerate(shapes):
        high, wide = min(rows, rows_most), min(columns, columns_most)
        if rows % high:
            high = rows
        if columns % wide:
            wide = columns
        for row in range(0, rows, high):
            for column in range(0, columns, wide):
                pieces.append((item, row, column, high, wide))
    return pieces


def slots_of(dims, sizes):
    return {
        dim: sum(sizes[other] - 1 for other in dims[: at]) for at, dim in enumerate(dims)
    }, sum(sizes[dim] - 1 for dim in dims)


def gather_kernel(dims, sizes, pieces, count, *refs):
    ins, outs = refs[:count], refs[count : 2 * count]
    send_sem, recv_sem, own_sem = refs[2 * count :]
    me = here(sizes)
    greet(me, sizes, dims)
    slot, _ = slots_of(dims, sizes)
    own = [
        pltpu.make_async_copy(
            ins[item], outs[item].at[tuple(me[dim] for dim in dims)], own_sem.at[item]
        )
        for item in range(count)
    ]
    for copy in own:
        copy.start()
    own_waited = set()

    def order_of(number):
        one, two = ("x", "y") if number % 2 == 0 else ("y", "x")
        order = (one, "z", two) if number % 3 == 1 else ("z", one, two)
        return [dim for dim in order + ("core",) if dim in dims]

    def region(number, stage, at):
        item, row, column, high, wide = pieces[number]
        done = order_of(number)[:stage]
        index = tuple(slice(None) if dim in done else at[dim] for dim in dims)
        return outs[item].at[index + (pl.ds(row, high), pl.ds(column, wide))]

    def copy_of(number, stage, step, source, target, device):
        place = slot[order_of(number)[stage]] + step - 1
        return pltpu.make_async_remote_copy(
            src_ref=source,
            dst_ref=target,
            send_sem=send_sem.at[number, place],
            recv_sem=recv_sem.at[number, place],
            device_id=device_of(device, sizes),
            device_id_type=MESH,
        )

    def receive(number, stage):
        dim = order_of(number)[stage]
        for step in range(1, sizes[dim]):
            giver = moved(me, sizes, dim, -step)
            landed = region(number, stage, giver)
            copy_of(number, stage, step, landed, landed, giver).wait_recv()

    sent = []
    depth = len(dims)
    for tick in range(len(pieces) + LAG * depth):
        for stage in range(depth + 1):
            number = tick - LAG * stage
            if not 0 <= number < len(pieces):
                continue
            item, row, column, high, wide = pieces[number]
            if stage > 0:
                receive(number, stage - 1)
            if stage == depth:
                continue
            if stage == 1 and item not in own_waited:
                own[item].wait()
                own_waited.add(item)
            dim = order_of(number)[stage]
            target = region(number, stage, me)
            source = target
            if stage == 0:
                source = ins[item].at[pl.ds(row, high), pl.ds(column, wide)]
            for step in range(1, sizes[dim]):
                copy = copy_of(
                    number, stage, step, source, target, moved(me, sizes, dim, step)
                )
                copy.start()
                sent.append(copy)
    for copy in sent:
        copy.wait_send()
    for item in range(count):
        if item not in own_waited:
            own[item].wait()


def gather_blocks(shards, dims, sizes, pieces, identity):
    count = len(shards)
    _, total = slots_of(dims, sizes)
    front = tuple(sizes[dim] for dim in dims)
    return pl.pallas_call(
        functools.partial(gather_kernel, dims, sizes, pieces, count),
        out_shape=[jax.ShapeDtypeStruct(front + s.shape, s.dtype) for s in shards],
        in_specs=[pl.BlockSpec(memory_space=pltpu.VMEM)] * count,
        out_specs=[pl.BlockSpec(memory_space=pl.ANY)] * count,
        scratch_shapes=[
            pltpu.SemaphoreType.DMA((len(pieces), total)),
            pltpu.SemaphoreType.DMA((len(pieces), total)),
            pltpu.SemaphoreType.DMA((count,)),
        ],
        compiler_params=pltpu.CompilerParams(collective_id=identity, has_side_effects=True),
    )(*shards)


def scatter_plan(number, dims):
    one, two = ("x", "y") if number % 2 == 0 else ("y", "x")
    order = (one, "z", two) if number % 3 == 2 else (one, two, "z")
    return [dim for dim in ("core",) + order if dim in dims]


def landing_shape(number, stage, dims, sizes, piece):
    order = scatter_plan(number, dims)
    left = tuple(sizes[dim] for dim in dims if dim not in order[: stage + 1])
    return (sizes[order[stage]] - 1,) + left + piece[3:]


def scatter_kernel(dims, sizes, pieces, count, *refs):
    ins, outs = refs[:count], refs[count : 2 * count]
    rest = list(refs[2 * count :])
    depth = len(dims)
    sums = rest[: len(pieces)]
    landing = [
        rest[len(pieces) + number * depth : len(pieces) + (number + 1) * depth]
        for number in range(len(pieces))
    ]
    send_sem, recv_sem, load_sem = rest[-3:]
    me = here(sizes)
    greet(me, sizes, dims)
    slot, _ = slots_of(dims, sizes)
    held = [dim for dim in dims if dim != "core"]

    def window(number, at):
        item, row, column, high, wide = pieces[number]
        index = tuple(at[dim] if dim == "core" else slice(None) for dim in dims)
        return ins[item].at[index + (pl.ds(row, high), pl.ds(column, wide))]

    loads = []
    for number in range(len(pieces)):
        load = pltpu.make_async_copy(window(number, me), sums[number], load_sem.at[number])
        load.start()
        loads.append(load)

    sent = []

    def copies(number, stage):
        dim = scatter_plan(number, dims)[stage]
        done = scatter_plan(number, dims)[:stage]
        made = []
        for step in range(1, sizes[dim]):
            peer = moved(me, sizes, dim, step)
            if dim == "core":
                source = window(number, peer)
            else:
                index = tuple(
                    peer[other] if other == dim else me[other] if other in done else slice(None)
                    for other in held
                )
                source = sums[number].at[index]
            place = slot[dim] + step - 1
            made.append(
                pltpu.make_async_remote_copy(
                    src_ref=source,
                    dst_ref=landing[number][stage].at[step - 1],
                    send_sem=send_sem.at[number, place],
                    recv_sem=recv_sem.at[number, place],
                    device_id=device_of(peer, sizes),
                    device_id_type=MESH,
                )
            )
        return made

    def reduce(number, stage):
        item, row, column, high, wide = pieces[number]
        order = scatter_plan(number, dims)
        left = [dim for dim in held if dim not in order[: stage + 1]]
        blocks = math.prod(sizes[dim] for dim in left)
        tile = min(high, BLOCK_ROWS)
        bands = high // tile

        def body(turn, carry):
            band = pl.ds(pl.multiple_of(lax.rem(turn, bands) * tile, tile), tile)
            block = turn // bands
            at = {}
            for dim in reversed(left):
                at[dim] = lax.rem(block, sizes[dim])
                block = block // sizes[dim]
            spot = tuple(at[dim] if dim in left else me[dim] for dim in held)
            value = sums[number][spot + (band, slice(None))].astype(jnp.float32)
            for step in range(1, sizes[order[stage]]):
                arrived = landing[number][stage][
                    (step - 1,) + tuple(at[dim] for dim in left) + (band, slice(None))
                ]
                value = value + arrived.astype(jnp.float32)
            if stage == depth - 1:
                start = pl.multiple_of(row + lax.rem(turn, bands) * tile, tile)
                outs[item][pl.ds(start, tile), pl.ds(column, wide)] = value
            else:
                sums[number][spot + (band, slice(None))] = value.astype(jnp.bfloat16)
            return carry

        lax.fori_loop(0, blocks * bands, body, 0)

    flights = {}

    def launch(number, stage):
        flights[number, stage] = copies(number, stage)
        for copy in flights[number, stage]:
            copy.start()
            sent.append(copy)

    if "core" in dims:
        for number in range(len(pieces)):
            launch(number, 0)
    first = 1 if "core" in dims else 0
    for tick in range(len(pieces) + LAG * depth):
        for stage in range(first, depth + 1):
            number = tick - LAG * (stage - first)
            if not 0 <= number < len(pieces):
                continue
            if stage == first:
                loads[number].wait()
            if stage > 0:
                for copy in flights[number, stage - 1]:
                    copy.wait_recv()
                reduce(number, stage - 1)
            if stage < depth:
                launch(number, stage)
    for copy in sent:
        copy.wait_send()


def scatter_blocks(blocks, dims, sizes, pieces, identity, limit):
    count = len(blocks)
    _, total = slots_of(dims, sizes)
    held = tuple(sizes[dim] for dim in dims if dim != "core")
    shapes = [b.shape[len(dims) :] for b in blocks]
    scratch = [pltpu.VMEM(held + piece[3:], jnp.bfloat16) for piece in pieces]
    for number, piece in enumerate(pieces):
        for stage in range(len(dims)):
            scratch.append(
                pltpu.VMEM(landing_shape(number, stage, dims, sizes, piece), jnp.bfloat16)
            )
    return pl.pallas_call(
        functools.partial(scatter_kernel, dims, sizes, pieces, count),
        out_shape=[jax.ShapeDtypeStruct(shape, jnp.float32) for shape in shapes],
        in_specs=[pl.BlockSpec(memory_space=pl.ANY)] * count,
        out_specs=[pl.BlockSpec(memory_space=pltpu.VMEM)] * count,
        scratch_shapes=scratch
        + [
            pltpu.SemaphoreType.DMA((len(pieces), total)),
            pltpu.SemaphoreType.DMA((len(pieces), total)),
            pltpu.SemaphoreType.DMA((len(pieces),)),
        ],
        compiler_params=pltpu.CompilerParams(
            collective_id=identity, has_side_effects=True, vmem_limit_bytes=limit
        ),
    )(*blocks)


ALL_DIMS = ("z", "core", "y", "x")
SEQ_DIMS = ("y", "x")


def tall(rows, columns):
    if rows % 16 == 0:
        return rows, columns
    return 16, rows * columns // 16


def gather_weights(matrices, vectors, sizes):
    count = math.prod(sizes[dim] for dim in ALL_DIMS)
    packed = jnp.concatenate(vectors)
    packed = jnp.pad(packed, (0, 2048 - packed.size)).reshape(16, 128)
    shards = [packed] + [m.reshape(tall(*m.shape)) for m in matrices]
    pieces = pieces_of([s.shape for s in shards], BLOCK_ROWS, BLOCK_COLUMNS)
    whole = gather_blocks(shards, ALL_DIMS, sizes, pieces, 0)
    flat = whole[0].reshape(count, 2048)
    parts, offset = [], 0
    for vector in vectors:
        parts.append(flat[:, offset : offset + vector.size].reshape(count * vector.size))
        offset += vector.size
    full = [
        w.reshape(count * m.shape[0], m.shape[1]) for w, m in zip(whole[1:], matrices)
    ]
    return full, parts


def scatter_grads(matrices, vectors, sizes):
    count = math.prod(sizes[dim] for dim in ALL_DIMS)
    front = tuple(sizes[dim] for dim in ALL_DIMS)
    packed = jnp.concatenate([v.reshape(count, -1) for v in vectors], axis=1)
    packed = jnp.pad(packed, ((0, 0), (0, 2048 - packed.shape[1]))).astype(jnp.bfloat16)
    blocks = [packed.reshape(front + (16, 128))]
    for matrix in matrices:
        shape = tall(matrix.shape[0] // count, matrix.shape[1])
        blocks.append(matrix.reshape(front + shape))
    pieces = pieces_of([b.shape[4:] for b in blocks], BLOCK_ROWS, BLOCK_COLUMNS)
    owned = scatter_blocks(blocks, ALL_DIMS, sizes, pieces, 1, 52 * 1024 * 1024)
    flat = owned[0].reshape(2048)
    parts, offset = [], 0
    for vector in vectors:
        part = vector.size // count
        parts.append(flat[offset : offset + part])
        offset += part
    full = [
        o.reshape(m.shape[0] // count, m.shape[1]) for o, m in zip(owned[1:], matrices)
    ]
    return full, parts


def gather_sequence(arrays, sizes):
    seqs, group, width = arrays[0].shape
    count = sizes["x"] * sizes["y"]
    shards = [a.reshape(seqs * group, width) for a in arrays]
    pieces = pieces_of([s.shape for s in shards], seqs * group, 512)
    whole = gather_blocks(shards, SEQ_DIMS, sizes, pieces, 2)
    return [
        jnp.moveaxis(w.reshape(count, seqs, group, width), 0, 1).reshape(
            seqs, count * group, width
        )
        for w in whole
    ]


def scatter_sequence(arrays, sizes):
    seqs, length, width = arrays[0].shape
    count = sizes["x"] * sizes["y"]
    group = length // count
    front = (sizes["y"], sizes["x"])
    blocks = [
        jnp.moveaxis(a.reshape(seqs, count, group, width), 1, 0).reshape(
            front + (seqs * group, width)
        )
        for a in arrays
    ]
    pieces = pieces_of([b.shape[2:] for b in blocks], seqs * group, 512)
    owned = scatter_blocks(blocks, SEQ_DIMS, sizes, pieces, 3, 52 * 1024 * 1024)
    return [o.reshape(seqs, group, width) for o in owned]


def layer_norm(values, gain, shift):
    centre = values - jnp.mean(values, axis=-1, keepdims=True)
    spread = jnp.mean(centre * centre, axis=-1, keepdims=True)
    return centre * lax.rsqrt(spread + 1e-05) * gain + shift


def gelu_tanh(values):
    return (
        0.5
        * values
        * (1.0 + jnp.tanh(0.7978845608028654 * (values + 0.044715 * values * values * values)))
    )


def rows_product(left, right):
    return jnp.dot(left, right, preferred_element_type=jnp.float32)


def weight_grad(left, right):
    return lax.dot_general(
        left, right, (((0,), (0,)), ((), ())), preferred_element_type=jnp.float32
    )


def input_grad(left, right):
    return lax.dot_general(
        left, right, (((1,), (1,)), ((), ())), preferred_element_type=jnp.float32
    )


def column_sum(values):
    return jnp.sum(values.astype(jnp.float32), axis=0)


def attend_kernel(query, key, value, mask, mixed):
    lane = lax.broadcasted_iota(jnp.int32, (1, query.shape[-1]), 1)
    total = jnp.zeros(query.shape[1:], jnp.float32)
    for head in range(query.shape[-1] // HEAD_DIM):
        own = (lane // HEAD_DIM == head).astype(jnp.bfloat16)
        scores = input_grad(query[0] * (own * 0.125), key[0])
        scores = jnp.where(mask[0] > 0, scores, -1e30)
        largest = jnp.max(scores, axis=-1, keepdims=True)
        expon = jnp.exp(scores - largest)
        scale = 1.0 / jnp.sum(expon, axis=-1, keepdims=True)
        probs = (expon * scale).astype(jnp.bfloat16)
        total = total + rows_product(probs, value[0] * own)
    mixed[0] = total.astype(jnp.bfloat16)


def attend_back_kernel(query, key, value, grad, mask, grad_query, grad_key, grad_value):
    lane = lax.broadcasted_iota(jnp.int32, (1, query.shape[-1]), 1)
    query_total = jnp.zeros(query.shape[1:], jnp.float32)
    key_total = jnp.zeros(key.shape[1:], jnp.float32)
    value_total = jnp.zeros(value.shape[1:], jnp.float32)
    for head in range(query.shape[-1] // HEAD_DIM):
        own = (lane // HEAD_DIM == head).astype(jnp.bfloat16)
        head_query = query[0] * (own * 0.125)
        head_grad = grad[0] * own
        scores = input_grad(key[0], head_query)
        scores = jnp.where(mask[0] > 0, scores, -1e30)
        largest = jnp.max(scores, axis=0, keepdims=True)
        expon = jnp.exp(scores - largest)
        probs = expon * (1.0 / jnp.sum(expon, axis=0, keepdims=True))
        grad_probs = input_grad(value[0], head_grad)
        centred = jnp.sum(probs * grad_probs, axis=0, keepdims=True)
        grad_scores = (probs * (grad_probs - centred)).astype(jnp.bfloat16)
        query_total = query_total + weight_grad(grad_scores, key[0] * own)
        key_total = key_total + rows_product(grad_scores, head_query)
        value_total = value_total + rows_product(probs.astype(jnp.bfloat16), head_grad)
    grad_query[0] = (query_total * 0.125).astype(jnp.bfloat16)
    grad_key[0] = key_total.astype(jnp.bfloat16)
    grad_value[0] = value_total.astype(jnp.bfloat16)


def pair_specs(lengths, mask_shape):
    specs = [pl.BlockSpec((1, length, 128), lambda b, h: (b, 0, h)) for length in lengths]
    return specs, pl.BlockSpec((1,) + mask_shape, lambda b, h: (b, 0, 0))


def attend(query, key, value, mask):
    seqs, group, width = query.shape
    length = key.shape[1]
    specs, mask_spec = pair_specs((group, length, length), (group, length))
    return pl.pallas_call(
        attend_kernel,
        grid=(seqs, width // 128),
        out_shape=jax.ShapeDtypeStruct(query.shape, jnp.bfloat16),
        in_specs=specs + [mask_spec],
        out_specs=specs[0],
        compiler_params=pltpu.CompilerParams(vmem_limit_bytes=40 * 1024 * 1024),
    )(query, key, value, mask)


def attend_back(query, key, value, grad, mask):
    seqs, group, width = query.shape
    length = key.shape[1]
    specs, mask_spec = pair_specs((group, length, length, group), (length, group))
    return pl.pallas_call(
        attend_back_kernel,
        grid=(seqs, width // 128),
        out_shape=[jax.ShapeDtypeStruct(a.shape, jnp.bfloat16) for a in (query, key, value)],
        in_specs=specs + [mask_spec],
        out_specs=specs[:3],
        compiler_params=pltpu.CompilerParams(vmem_limit_bytes=48 * 1024 * 1024),
    )(query, key, value, grad, mask)


def local(
    inputs,
    segments,
    cotangent,
    first_gain,
    first_shift,
    qkv_weight,
    query_bias,
    value_bias,
    output_weight,
    output_bias,
    second_gain,
    second_shift,
    expand_weight,
    expand_bias,
    shrink_weight,
    shrink_bias,
):
    sizes = lattice(lax.axis_size("fsdp"), lax.axis_size("seq"))
    matrices, vectors = gather_weights(
        (qkv_weight, output_weight, expand_weight, shrink_weight),
        (
            first_gain,
            first_shift,
            query_bias,
            value_bias,
            output_bias,
            second_gain,
            second_shift,
            expand_bias,
            shrink_bias,
        ),
        sizes,
    )
    qkv_full, output_full, expand_full, shrink_full = matrices
    forward_set = (
        vectors[0],
        vectors[1],
        qkv_full,
        vectors[2],
        vectors[3],
        output_full,
        vectors[4],
        vectors[5],
        vectors[6],
        expand_full,
        vectors[7],
        shrink_full,
        vectors[8],
    )
    seqs, group, width = inputs.shape
    length = segments.shape[1]
    rows = seqs * group
    gain_first = forward_set[0].astype(jnp.float32)
    shift_first = forward_set[1].astype(jnp.float32)
    gain_second = forward_set[7].astype(jnp.float32)
    shift_second = forward_set[8].astype(jnp.float32)
    tokens = inputs.reshape(rows, width).astype(jnp.float32)
    acts_first = layer_norm(tokens, gain_first, shift_first).astype(jnp.bfloat16)
    joined = rows_product(acts_first, forward_set[2])
    query_rows = (joined[:, :width] + forward_set[3].astype(jnp.float32)).astype(jnp.bfloat16)
    key_local = joined[:, width : 2 * width].astype(jnp.bfloat16).reshape(seqs, group, width)
    value_local = (
        (joined[:, 2 * width :] + forward_set[4].astype(jnp.float32))
        .astype(jnp.bfloat16)
        .reshape(seqs, group, width)
    )
    key_all, value_all = gather_sequence((key_local, value_local), sizes)
    first_place = lax.axis_index("seq") * group
    query_segment = lax.dynamic_slice_in_dim(segments, first_place, group, 1)
    query_place = first_place + jnp.arange(group)
    key_place = jnp.arange(length)
    causal = key_place[None, :] <= query_place[:, None]
    allowed = causal[None] & (query_segment[:, :, None] == segments[:, None, :])
    allowed = allowed.astype(jnp.float32)
    queries = query_rows.reshape(seqs, group, width)
    mixed = attend(queries, key_all, value_all, allowed).reshape(rows, width)
    middle = tokens + rows_product(mixed, forward_set[5]) + forward_set[6].astype(jnp.float32)
    acts_second = layer_norm(middle, gain_second, shift_second).astype(jnp.bfloat16)
    hidden_pre = rows_product(acts_second, forward_set[9]) + forward_set[10].astype(jnp.float32)
    acts_third = gelu_tanh(hidden_pre).astype(jnp.bfloat16)
    result = (
        middle + rows_product(acts_third, forward_set[11]) + forward_set[12].astype(jnp.float32)
    )
    outputs = result.astype(jnp.bfloat16).reshape(seqs, group, width)
    back_set = forward_set
    grad_out = cotangent.reshape(rows, width)
    grad_shrink = weight_grad(acts_third, grad_out)
    grad_shrink_bias = column_sum(grad_out)
    grad_hidden = input_grad(grad_out, back_set[11])
    gelu_value, gelu_pull = jax.vjp(gelu_tanh, hidden_pre)
    grad_pre = gelu_pull(grad_hidden)[0].astype(jnp.bfloat16)
    grad_expand = weight_grad(acts_second, grad_pre)
    grad_expand_bias = column_sum(grad_pre)
    grad_acts_second = input_grad(grad_pre, back_set[9])
    norm_value, second_pull = jax.vjp(
        layer_norm, middle, back_set[7].astype(jnp.float32), back_set[8].astype(jnp.float32)
    )
    grad_middle_norm, grad_gain_second, grad_shift_second = second_pull(grad_acts_second)
    grad_middle = grad_out.astype(jnp.float32) + grad_middle_norm
    grad_branch = grad_middle.astype(jnp.bfloat16)
    grad_output = weight_grad(mixed, grad_branch)
    grad_output_bias = column_sum(grad_branch)
    grad_mixed = (
        input_grad(grad_branch, back_set[5]).astype(jnp.bfloat16).reshape(seqs, group, width)
    )
    grad_query, key_terms, value_terms = attend_back(
        queries, key_all, value_all, grad_mixed, allowed.swapaxes(1, 2)
    )
    grad_key, grad_value = scatter_sequence(
        (key_terms, value_terms),
        sizes,
    )
    grad_joined = jnp.concatenate(
        [
            grad_query.reshape(rows, width),
            grad_key.reshape(rows, width).astype(jnp.bfloat16),
            grad_value.reshape(rows, width).astype(jnp.bfloat16),
        ],
        axis=1,
    )
    grad_qkv = weight_grad(acts_first, grad_joined)
    grad_query_bias = column_sum(grad_joined[:, :width])
    grad_value_bias = column_sum(grad_joined[:, 2 * width :])
    grad_acts_first = input_grad(grad_joined, back_set[2])
    first_value, first_pull = jax.vjp(
        layer_norm, tokens, back_set[0].astype(jnp.float32), back_set[1].astype(jnp.float32)
    )
    grad_tokens_norm, grad_gain_first, grad_shift_first = first_pull(grad_acts_first)
    grad_inputs = (grad_middle + grad_tokens_norm).astype(jnp.bfloat16).reshape(seqs, group, width)
    owned, parts = scatter_grads(
        tuple(
            grad.astype(jnp.bfloat16)
            for grad in (grad_qkv, grad_output, grad_expand, grad_shrink)
        ),
        (
            grad_gain_first,
            grad_shift_first,
            grad_query_bias,
            grad_value_bias,
            grad_output_bias,
            grad_gain_second,
            grad_shift_second,
            grad_expand_bias,
            grad_shrink_bias,
        ),
        sizes,
    )
    return (
        outputs,
        grad_inputs,
        parts[0],
        parts[1],
        owned[0],
        parts[2],
        parts[3],
        owned[1],
        parts[4],
        parts[5],
        parts[6],
        owned[2],
        parts[7],
        owned[3],
        parts[8],
    )


def solution(mesh):
    placed = (
        P("fsdp", "seq", None),
        P("fsdp", None),
        P("fsdp", "seq", None),
        P(("fsdp", "seq")),
        P(("fsdp", "seq")),
        P(("fsdp", "seq"), None),
        P(("fsdp", "seq")),
        P(("fsdp", "seq")),
        P(("fsdp", "seq"), None),
        P(("fsdp", "seq")),
        P(("fsdp", "seq")),
        P(("fsdp", "seq")),
        P(("fsdp", "seq"), None),
        P(("fsdp", "seq")),
        P(("fsdp", "seq"), None),
        P(("fsdp", "seq")),
    )
    return jax.shard_map(
        local,
        mesh=mesh,
        in_specs=placed,
        out_specs=(
            P("fsdp", "seq", None),
            P("fsdp", "seq", None),
            P(("fsdp", "seq")),
            P(("fsdp", "seq")),
            P(("fsdp", "seq"), None),
            P(("fsdp", "seq")),
            P(("fsdp", "seq")),
            P(("fsdp", "seq"), None),
            P(("fsdp", "seq")),
            P(("fsdp", "seq")),
            P(("fsdp", "seq")),
            P(("fsdp", "seq"), None),
            P(("fsdp", "seq")),
            P(("fsdp", "seq"), None),
            P(("fsdp", "seq")),
        ),
        check_vma=False,
    )
```

```python
import functools
import math

import jax
import jax.numpy as jnp
from jax import lax
from jax.experimental import pallas as pl
from jax.experimental.pallas import tpu as pltpu
from jax.sharding import PartitionSpec as P

HEAD_DIM = 64

BLOCK_ROWS = 32
BLOCK_COLUMNS = 512
LAG = 2
MESH = pl.DeviceIdType.MESH


def lattice(group_count, place_count):
    side = math.isqrt(place_count)
    return {"z": group_count // 2, "core": 2, "y": place_count // side, "x": side}


def here(sizes):
    group, place = lax.axis_index("fsdp"), lax.axis_index("seq")
    return {
        "z": group // 2,
        "core": lax.rem(group, 2),
        "y": place // sizes["x"],
        "x": lax.rem(place, sizes["x"]),
    }


def moved(me, sizes, dim, step):
    other = dict(me)
    other[dim] = lax.rem(me[dim] + step + sizes[dim], sizes[dim])
    return other


def device_of(at, sizes):
    return {"fsdp": at["z"] * 2 + at["core"], "seq": at["y"] * sizes["x"] + at["x"]}


def greet(me, sizes, dims):
    barrier = pltpu.get_barrier_semaphore()
    count = 0
    for dim in dims:
        for step in range(1, sizes[dim]):
            pl.semaphore_signal(
                barrier,
                inc=1,
                device_id=device_of(moved(me, sizes, dim, step), sizes),
                device_id_type=MESH,
            )
            count += 1
    pl.semaphore_wait(barrier, count)


def pieces_of(shapes, rows_most, columns_most):
    pieces = []
    for item, (rows, columns) in enumerate(shapes):
        high, wide = min(rows, rows_most), min(columns, columns_most)
        if rows % high:
            high = rows
        if columns % wide:
            wide = columns
        for row in range(0, rows, high):
            for column in range(0, columns, wide):
                pieces.append((item, row, column, high, wide))
    return pieces


def slots_of(dims, sizes):
    return {
        dim: sum(sizes[other] - 1 for other in dims[: at]) for at, dim in enumerate(dims)
    }, sum(sizes[dim] - 1 for dim in dims)


def gather_kernel(dims, sizes, pieces, count, *refs):
    ins, outs = refs[:count], refs[count : 2 * count]
    send_sem, recv_sem, own_sem = refs[2 * count :]
    me = here(sizes)
    greet(me, sizes, dims)
    slot, _ = slots_of(dims, sizes)
    own = [
        pltpu.make_async_copy(
            ins[item], outs[item].at[tuple(me[dim] for dim in dims)], own_sem.at[item]
        )
        for item in range(count)
    ]
    for copy in own:
        copy.start()
    own_waited = set()

    def order_of(number):
        one, two = ("x", "y") if number % 2 == 0 else ("y", "x")
        order = (one, "z", two) if number % 3 == 1 else ("z", one, two)
        return [dim for dim in order + ("core",) if dim in dims]

    def region(number, stage, at):
        item, row, column, high, wide = pieces[number]
        done = order_of(number)[:stage]
        index = tuple(slice(None) if dim in done else at[dim] for dim in dims)
        return outs[item].at[index + (pl.ds(row, high), pl.ds(column, wide))]

    def copy_of(number, stage, step, source, target, device):
        place = slot[order_of(number)[stage]] + step - 1
        return pltpu.make_async_remote_copy(
            src_ref=source,
            dst_ref=target,
            send_sem=send_sem.at[number, place],
            recv_sem=recv_sem.at[number, place],
            device_id=device_of(device, sizes),
            device_id_type=MESH,
        )

    def receive(number, stage):
        dim = order_of(number)[stage]
        for step in range(1, sizes[dim]):
            giver = moved(me, sizes, dim, -step)
            landed = region(number, stage, giver)
            copy_of(number, stage, step, landed, landed, giver).wait_recv()

    sent = []
    depth = len(dims)
    for tick in range(len(pieces) + LAG * depth):
        for stage in range(depth + 1):
            number = tick - LAG * stage
            if not 0 <= number < len(pieces):
                continue
            item, row, column, high, wide = pieces[number]
            if stage > 0:
                receive(number, stage - 1)
            if stage == depth:
                continue
            if stage == 1 and item not in own_waited:
                own[item].wait()
                own_waited.add(item)
            dim = order_of(number)[stage]
            target = region(number, stage, me)
            source = target
            if stage == 0:
                source = ins[item].at[pl.ds(row, high), pl.ds(column, wide)]
            for step in range(1, sizes[dim]):
                copy = copy_of(
                    number, stage, step, source, target, moved(me, sizes, dim, step)
                )
                copy.start()
                sent.append(copy)
    for copy in sent:
        copy.wait_send()
    for item in range(count):
        if item not in own_waited:
            own[item].wait()


def gather_blocks(shards, dims, sizes, pieces, identity):
    count = len(shards)
    _, total = slots_of(dims, sizes)
    front = tuple(sizes[dim] for dim in dims)
    return pl.pallas_call(
        functools.partial(gather_kernel, dims, sizes, pieces, count),
        out_shape=[jax.ShapeDtypeStruct(front + s.shape, s.dtype) for s in shards],
        in_specs=[pl.BlockSpec(memory_space=pltpu.VMEM)] * count,
        out_specs=[pl.BlockSpec(memory_space=pl.ANY)] * count,
        scratch_shapes=[
            pltpu.SemaphoreType.DMA((len(pieces), total)),
            pltpu.SemaphoreType.DMA((len(pieces), total)),
            pltpu.SemaphoreType.DMA((count,)),
        ],
        compiler_params=pltpu.CompilerParams(collective_id=identity, has_side_effects=True),
    )(*shards)


def scatter_plan(number, dims):
    one, two = ("x", "y") if number % 2 == 0 else ("y", "x")
    order = (one, "z", two) if number % 3 == 2 else (one, two, "z")
    return [dim for dim in ("core",) + order if dim in dims]


def landing_shape(number, stage, dims, sizes, piece):
    order = scatter_plan(number, dims)
    left = tuple(sizes[dim] for dim in dims if dim not in order[: stage + 1])
    return (sizes[order[stage]] - 1,) + left + piece[3:]


def scatter_kernel(dims, sizes, pieces, count, *refs):
    ins, outs = refs[:count], refs[count : 2 * count]
    rest = list(refs[2 * count :])
    depth = len(dims)
    sums = rest[: len(pieces)]
    landing = [
        rest[len(pieces) + number * depth : len(pieces) + (number + 1) * depth]
        for number in range(len(pieces))
    ]
    send_sem, recv_sem, load_sem = rest[-3:]
    me = here(sizes)
    greet(me, sizes, dims)
    slot, _ = slots_of(dims, sizes)
    held = [dim for dim in dims if dim != "core"]

    def window(number, at):
        item, row, column, high, wide = pieces[number]
        index = tuple(at[dim] if dim == "core" else slice(None) for dim in dims)
        return ins[item].at[index + (pl.ds(row, high), pl.ds(column, wide))]

    loads = []
    for number in range(len(pieces)):
        load = pltpu.make_async_copy(window(number, me), sums[number], load_sem.at[number])
        load.start()
        loads.append(load)

    sent = []

    def copies(number, stage):
        dim = scatter_plan(number, dims)[stage]
        done = scatter_plan(number, dims)[:stage]
        made = []
        for step in range(1, sizes[dim]):
            peer = moved(me, sizes, dim, step)
            if dim == "core":
                source = window(number, peer)
            else:
                index = tuple(
                    peer[other] if other == dim else me[other] if other in done else slice(None)
                    for other in held
                )
                source = sums[number].at[index]
            place = slot[dim] + step - 1
            made.append(
                pltpu.make_async_remote_copy(
                    src_ref=source,
                    dst_ref=landing[number][stage].at[step - 1],
                    send_sem=send_sem.at[number, place],
                    recv_sem=recv_sem.at[number, place],
                    device_id=device_of(peer, sizes),
                    device_id_type=MESH,
                )
            )
        return made

    def reduce(number, stage):
        item, row, column, high, wide = pieces[number]
        order = scatter_plan(number, dims)
        left = [dim for dim in held if dim not in order[: stage + 1]]
        blocks = math.prod(sizes[dim] for dim in left)
        tile = min(high, BLOCK_ROWS)
        bands = high // tile

        def body(turn, carry):
            band = pl.ds(pl.multiple_of(lax.rem(turn, bands) * tile, tile), tile)
            block = turn // bands
            at = {}
            for dim in reversed(left):
                at[dim] = lax.rem(block, sizes[dim])
                block = block // sizes[dim]
            spot = tuple(at[dim] if dim in left else me[dim] for dim in held)
            value = sums[number][spot + (band, slice(None))].astype(jnp.float32)
            for step in range(1, sizes[order[stage]]):
                arrived = landing[number][stage][
                    (step - 1,) + tuple(at[dim] for dim in left) + (band, slice(None))
                ]
                value = value + arrived.astype(jnp.float32)
            if stage == depth - 1:
                start = pl.multiple_of(row + lax.rem(turn, bands) * tile, tile)
                outs[item][pl.ds(start, tile), pl.ds(column, wide)] = value
            else:
                sums[number][spot + (band, slice(None))] = value.astype(jnp.bfloat16)
            return carry

        lax.fori_loop(0, blocks * bands, body, 0)

    flights = {}

    def launch(number, stage):
        flights[number, stage] = copies(number, stage)
        for copy in flights[number, stage]:
            copy.start()
            sent.append(copy)

    if "core" in dims:
        for number in range(len(pieces)):
            launch(number, 0)
    first = 1 if "core" in dims else 0
    for tick in range(len(pieces) + LAG * depth):
        for stage in range(first, depth + 1):
            number = tick - LAG * (stage - first)
            if not 0 <= number < len(pieces):
                continue
            if stage == first:
                loads[number].wait()
            if stage > 0:
                for copy in flights[number, stage - 1]:
                    copy.wait_recv()
                reduce(number, stage - 1)
            if stage < depth:
                launch(number, stage)
    for copy in sent:
        copy.wait_send()


def scatter_blocks(blocks, dims, sizes, pieces, identity, limit):
    count = len(blocks)
    _, total = slots_of(dims, sizes)
    held = tuple(sizes[dim] for dim in dims if dim != "core")
    shapes = [b.shape[len(dims) :] for b in blocks]
    scratch = [pltpu.VMEM(held + piece[3:], jnp.bfloat16) for piece in pieces]
    for number, piece in enumerate(pieces):
        for stage in range(len(dims)):
            scratch.append(
                pltpu.VMEM(landing_shape(number, stage, dims, sizes, piece), jnp.bfloat16)
            )
    return pl.pallas_call(
        functools.partial(scatter_kernel, dims, sizes, pieces, count),
        out_shape=[jax.ShapeDtypeStruct(shape, jnp.float32) for shape in shapes],
        in_specs=[pl.BlockSpec(memory_space=pl.ANY)] * count,
        out_specs=[pl.BlockSpec(memory_space=pltpu.VMEM)] * count,
        scratch_shapes=scratch
        + [
            pltpu.SemaphoreType.DMA((len(pieces), total)),
            pltpu.SemaphoreType.DMA((len(pieces), total)),
            pltpu.SemaphoreType.DMA((len(pieces),)),
        ],
        compiler_params=pltpu.CompilerParams(
            collective_id=identity, has_side_effects=True, vmem_limit_bytes=limit
        ),
    )(*blocks)


ALL_DIMS = ("z", "core", "y", "x")
SEQ_DIMS = ("y", "x")


def tall(rows, columns):
    if rows % 16 == 0:
        return rows, columns
    return 16, rows * columns // 16


def gather_weights(matrices, vectors, sizes):
    count = math.prod(sizes[dim] for dim in ALL_DIMS)
    packed = jnp.concatenate(vectors)
    packed = jnp.pad(packed, (0, 2048 - packed.size)).reshape(16, 128)
    shards = [packed] + [m.reshape(tall(*m.shape)) for m in matrices]
    pieces = pieces_of([s.shape for s in shards], BLOCK_ROWS, BLOCK_COLUMNS)
    whole = gather_blocks(shards, ALL_DIMS, sizes, pieces, 0)
    flat = whole[0].reshape(count, 2048)
    parts, offset = [], 0
    for vector in vectors:
        parts.append(flat[:, offset : offset + vector.size].reshape(count * vector.size))
        offset += vector.size
    full = [
        w.reshape(count * m.shape[0], m.shape[1]) for w, m in zip(whole[1:], matrices)
    ]
    return full, parts


def scatter_grads(matrices, vectors, sizes):
    count = math.prod(sizes[dim] for dim in ALL_DIMS)
    front = tuple(sizes[dim] for dim in ALL_DIMS)
    packed = jnp.concatenate([v.reshape(count, -1) for v in vectors], axis=1)
    packed = jnp.pad(packed, ((0, 0), (0, 2048 - packed.shape[1]))).astype(jnp.bfloat16)
    blocks = [packed.reshape(front + (16, 128))]
    for matrix in matrices:
        shape = tall(matrix.shape[0] // count, matrix.shape[1])
        blocks.append(matrix.reshape(front + shape))
    pieces = pieces_of([b.shape[4:] for b in blocks], BLOCK_ROWS, BLOCK_COLUMNS)
    owned = scatter_blocks(blocks, ALL_DIMS, sizes, pieces, 1, 52 * 1024 * 1024)
    flat = owned[0].reshape(2048)
    parts, offset = [], 0
    for vector in vectors:
        part = vector.size // count
        parts.append(flat[offset : offset + part])
        offset += part
    full = [
        o.reshape(m.shape[0] // count, m.shape[1]) for o, m in zip(owned[1:], matrices)
    ]
    return full, parts


def gather_sequence(arrays, sizes):
    seqs, group, width = arrays[0].shape
    count = sizes["x"] * sizes["y"]
    shards = [a.reshape(seqs * group, width) for a in arrays]
    pieces = pieces_of([s.shape for s in shards], seqs * group, 512)
    whole = gather_blocks(shards, SEQ_DIMS, sizes, pieces, 2)
    return [
        jnp.moveaxis(w.reshape(count, seqs, group, width), 0, 1).reshape(
            seqs, count * group, width
        )
        for w in whole
    ]


def scatter_sequence(arrays, sizes):
    seqs, length, width = arrays[0].shape
    count = sizes["x"] * sizes["y"]
    group = length // count
    front = (sizes["y"], sizes["x"])
    blocks = [
        jnp.moveaxis(a.reshape(seqs, count, group, width), 1, 0).reshape(
            front + (seqs * group, width)
        )
        for a in arrays
    ]
    pieces = pieces_of([b.shape[2:] for b in blocks], seqs * group, 512)
    owned = scatter_blocks(blocks, SEQ_DIMS, sizes, pieces, 3, 52 * 1024 * 1024)
    return [o.reshape(seqs, group, width) for o in owned]


def layer_norm(values, gain, shift):
    centre = values - jnp.mean(values, axis=-1, keepdims=True)
    spread = jnp.mean(centre * centre, axis=-1, keepdims=True)
    return centre * lax.rsqrt(spread + 1e-05) * gain + shift


def gelu_tanh(values):
    return (
        0.5
        * values
        * (1.0 + jnp.tanh(0.7978845608028654 * (values + 0.044715 * values * values * values)))
    )


def rows_product(left, right):
    return jnp.dot(left, right, preferred_element_type=jnp.float32)


def weight_grad(left, right):
    return lax.dot_general(
        left, right, (((0,), (0,)), ((), ())), preferred_element_type=jnp.float32
    )


def input_grad(left, right):
    return lax.dot_general(
        left, right, (((1,), (1,)), ((), ())), preferred_element_type=jnp.float32
    )


def column_sum(values):
    return jnp.sum(values.astype(jnp.float32), axis=0)


def attend_kernel(query, key, value, mask, mixed):
    lane = lax.broadcasted_iota(jnp.int32, (1, query.shape[-1]), 1)
    total = jnp.zeros(query.shape[1:], jnp.float32)
    for head in range(query.shape[-1] // HEAD_DIM):
        own = (lane // HEAD_DIM == head).astype(jnp.bfloat16)
        scores = input_grad(query[0] * (own * 0.125), key[0])
        scores = jnp.where(mask[0] > 0, scores, -1e30)
        largest = jnp.max(scores, axis=-1, keepdims=True)
        expon = jnp.exp(scores - largest)
        scale = 1.0 / jnp.sum(expon, axis=-1, keepdims=True)
        probs = (expon * scale).astype(jnp.bfloat16)
        total = total + rows_product(probs, value[0] * own)
    mixed[0] = total.astype(jnp.bfloat16)


def attend_back_kernel(query, key, value, grad, mask, grad_query, grad_key, grad_value):
    lane = lax.broadcasted_iota(jnp.int32, (1, query.shape[-1]), 1)
    query_total = jnp.zeros(query.shape[1:], jnp.float32)
    key_total = jnp.zeros(key.shape[1:], jnp.float32)
    value_total = jnp.zeros(value.shape[1:], jnp.float32)
    for head in range(query.shape[-1] // HEAD_DIM):
        own = (lane // HEAD_DIM == head).astype(jnp.bfloat16)
        head_query = query[0] * (own * 0.125)
        head_grad = grad[0] * own
        scores = input_grad(key[0], head_query)
        scores = jnp.where(mask[0] > 0, scores, -1e30)
        largest = jnp.max(scores, axis=0, keepdims=True)
        expon = jnp.exp(scores - largest)
        probs = expon * (1.0 / jnp.sum(expon, axis=0, keepdims=True))
        grad_probs = input_grad(value[0], head_grad)
        centred = jnp.sum(probs * grad_probs, axis=0, keepdims=True)
        grad_scores = (probs * (grad_probs - centred)).astype(jnp.bfloat16)
        query_total = query_total + weight_grad(grad_scores, key[0] * own)
        key_total = key_total + rows_product(grad_scores, head_query)
        value_total = value_total + rows_product(probs.astype(jnp.bfloat16), head_grad)
    grad_query[0] = (query_total * 0.125).astype(jnp.bfloat16)
    grad_key[0] = key_total.astype(jnp.bfloat16)
    grad_value[0] = value_total.astype(jnp.bfloat16)


def pair_specs(lengths, mask_shape):
    specs = [pl.BlockSpec((1, length, 128), lambda b, h: (b, 0, h)) for length in lengths]
    return specs, pl.BlockSpec((1,) + mask_shape, lambda b, h: (b, 0, 0))


def attend(query, key, value, mask):
    seqs, group, width = query.shape
    length = key.shape[1]
    specs, mask_spec = pair_specs((group, length, length), (group, length))
    return pl.pallas_call(
        attend_kernel,
        grid=(seqs, width // 128),
        out_shape=jax.ShapeDtypeStruct(query.shape, jnp.bfloat16),
        in_specs=specs + [mask_spec],
        out_specs=specs[0],
        compiler_params=pltpu.CompilerParams(vmem_limit_bytes=40 * 1024 * 1024),
    )(query, key, value, mask)


def attend_back(query, key, value, grad, mask):
    seqs, group, width = query.shape
    length = key.shape[1]
    specs, mask_spec = pair_specs((group, length, length, group), (length, group))
    return pl.pallas_call(
        attend_back_kernel,
        grid=(seqs, width // 128),
        out_shape=[jax.ShapeDtypeStruct(a.shape, jnp.bfloat16) for a in (query, key, value)],
        in_specs=specs + [mask_spec],
        out_specs=specs[:3],
        compiler_params=pltpu.CompilerParams(vmem_limit_bytes=48 * 1024 * 1024),
    )(query, key, value, grad, mask)


def local(
    inputs,
    segments,
    cotangent,
    first_gain,
    first_shift,
    qkv_weight,
    query_bias,
    value_bias,
    output_weight,
    output_bias,
    second_gain,
    second_shift,
    expand_weight,
    expand_bias,
    shrink_weight,
    shrink_bias,
):
    sizes = lattice(lax.axis_size("fsdp"), lax.axis_size("seq"))
    matrices, vectors = gather_weights(
        (qkv_weight, output_weight, expand_weight, shrink_weight),
        (
            first_gain,
            first_shift,
            query_bias,
            value_bias,
            output_bias,
            second_gain,
            second_shift,
            expand_bias,
            shrink_bias,
        ),
        sizes,
    )
    qkv_full, output_full, expand_full, shrink_full = matrices
    forward_set = (
        vectors[0],
        vectors[1],
        qkv_full,
        vectors[2],
        vectors[3],
        output_full,
        vectors[4],
        vectors[5],
        vectors[6],
        expand_full,
        vectors[7],
        shrink_full,
        vectors[8],
    )
    seqs, group, width = inputs.shape
    length = segments.shape[1]
    rows = seqs * group
    gain_first = forward_set[0].astype(jnp.float32)
    shift_first = forward_set[1].astype(jnp.float32)
    gain_second = forward_set[7].astype(jnp.float32)
    shift_second = forward_set[8].astype(jnp.float32)
    tokens = inputs.reshape(rows, width).astype(jnp.float32)
    acts_first = layer_norm(tokens, gain_first, shift_first).astype(jnp.bfloat16)
    joined = rows_product(acts_first, forward_set[2])
    query_rows = (joined[:, :width] + forward_set[3].astype(jnp.float32)).astype(jnp.bfloat16)
    key_local = joined[:, width : 2 * width].astype(jnp.bfloat16).reshape(seqs, group, width)
    value_local = (
        (joined[:, 2 * width :] + forward_set[4].astype(jnp.float32))
        .astype(jnp.bfloat16)
        .reshape(seqs, group, width)
    )
    key_all, value_all = gather_sequence((key_local, value_local), sizes)
    first_place = lax.axis_index("seq") * group
    query_segment = lax.dynamic_slice_in_dim(segments, first_place, group, 1)
    query_place = first_place + jnp.arange(group)
    key_place = jnp.arange(length)
    causal = key_place[None, :] <= query_place[:, None]
    allowed = causal[None] & (query_segment[:, :, None] == segments[:, None, :])
    allowed = allowed.astype(jnp.float32)
    queries = query_rows.reshape(seqs, group, width)
    mixed = attend(queries, key_all, value_all, allowed).reshape(rows, width)
    middle = tokens + rows_product(mixed, forward_set[5]) + forward_set[6].astype(jnp.float32)
    acts_second = layer_norm(middle, gain_second, shift_second).astype(jnp.bfloat16)
    hidden_pre = rows_product(acts_second, forward_set[9]) + forward_set[10].astype(jnp.float32)
    acts_third = gelu_tanh(hidden_pre).astype(jnp.bfloat16)
    result = (
        middle + rows_product(acts_third, forward_set[11]) + forward_set[12].astype(jnp.float32)
    )
    outputs = result.astype(jnp.bfloat16).reshape(seqs, group, width)
    back_set = forward_set
    grad_out = cotangent.reshape(rows, width)
    grad_shrink = weight_grad(acts_third, grad_out)
    grad_shrink_bias = column_sum(grad_out)
    grad_hidden = input_grad(grad_out, back_set[11])
    gelu_value, gelu_pull = jax.vjp(gelu_tanh, hidden_pre)
    grad_pre = gelu_pull(grad_hidden)[0].astype(jnp.bfloat16)
    grad_expand = weight_grad(acts_second, grad_pre)
    grad_expand_bias = column_sum(grad_pre)
    grad_acts_second = input_grad(grad_pre, back_set[9])
    norm_value, second_pull = jax.vjp(
        layer_norm, middle, back_set[7].astype(jnp.float32), back_set[8].astype(jnp.float32)
    )
    grad_middle_norm, grad_gain_second, grad_shift_second = second_pull(grad_acts_second)
    grad_middle = grad_out.astype(jnp.float32) + grad_middle_norm
    grad_branch = grad_middle.astype(jnp.bfloat16)
    grad_output = weight_grad(mixed, grad_branch)
    grad_output_bias = column_sum(grad_branch)
    grad_mixed = (
        input_grad(grad_branch, back_set[5]).astype(jnp.bfloat16).reshape(seqs, group, width)
    )
    grad_query, key_terms, value_terms = attend_back(
        queries, key_all, value_all, grad_mixed, allowed.swapaxes(1, 2)
    )
    grad_key, grad_value = scatter_sequence(
        (key_terms, value_terms),
        sizes,
    )
    grad_joined = jnp.concatenate(
        [
            grad_query.reshape(rows, width),
            grad_key.reshape(rows, width).astype(jnp.bfloat16),
            grad_value.reshape(rows, width).astype(jnp.bfloat16),
        ],
        axis=1,
    )
    grad_qkv = weight_grad(acts_first, grad_joined)
    grad_query_bias = column_sum(grad_joined[:, :width])
    grad_value_bias = column_sum(grad_joined[:, 2 * width :])
    grad_acts_first = input_grad(grad_joined, back_set[2])
    first_value, first_pull = jax.vjp(
        layer_norm, tokens, back_set[0].astype(jnp.float32), back_set[1].astype(jnp.float32)
    )
    grad_tokens_norm, grad_gain_first, grad_shift_first = first_pull(grad_acts_first)
    grad_inputs = (grad_middle + grad_tokens_norm).astype(jnp.bfloat16).reshape(seqs, group, width)
    owned, parts = scatter_grads(
        tuple(
            grad.astype(jnp.bfloat16)
            for grad in (grad_qkv, grad_output, grad_expand, grad_shrink)
        ),
        (
            grad_gain_first,
            grad_shift_first,
            grad_query_bias,
            grad_value_bias,
            grad_output_bias,
            grad_gain_second,
            grad_shift_second,
            grad_expand_bias,
            grad_shrink_bias,
        ),
        sizes,
    )
    return (
        outputs,
        grad_inputs,
        parts[0],
        parts[1],
        owned[0],
        parts[2],
        parts[3],
        owned[1],
        parts[4],
        parts[5],
        parts[6],
        owned[2],
        parts[7],
        owned[3],
        parts[8],
    )


def solution(mesh):
    placed = (
        P("fsdp", "seq", None),
        P("fsdp", None),
        P("fsdp", "seq", None),
        P(("fsdp", "seq")),
        P(("fsdp", "seq")),
        P(("fsdp", "seq"), None),
        P(("fsdp", "seq")),
        P(("fsdp", "seq")),
        P(("fsdp", "seq"), None),
        P(("fsdp", "seq")),
        P(("fsdp", "seq")),
        P(("fsdp", "seq")),
        P(("fsdp", "seq"), None),
        P(("fsdp", "seq")),
        P(("fsdp", "seq"), None),
        P(("fsdp", "seq")),
    )
    return jax.shard_map(
        local,
        mesh=mesh,
        in_specs=placed,
        out_specs=(
            P("fsdp", "seq", None),
            P("fsdp", "seq", None),
            P(("fsdp", "seq")),
            P(("fsdp", "seq")),
            P(("fsdp", "seq"), None),
            P(("fsdp", "seq")),
            P(("fsdp", "seq")),
            P(("fsdp", "seq"), None),
            P(("fsdp", "seq")),
            P(("fsdp", "seq")),
            P(("fsdp", "seq")),
            P(("fsdp", "seq"), None),
            P(("fsdp", "seq")),
            P(("fsdp", "seq"), None),
            P(("fsdp", "seq")),
        ),
        check_vma=False,
    )
```
